256 devices in a mesh: gz: 8 (over y, x_lo), row: 4 (over x_hi, core), col: 8 (over z).
Axes of the slice: x: 4 (x_hi: 2, x_lo: 2; x = x_hi * 2 + x_lo), y: 4, z: 8, core: 2. Of those that a mesh axis runs over, the one named last changes fastest.
Arguments:
- sections: bfloat16 [16, 2048, 4096], P('gz', 'row', 'col'), may hold values from -6 to 6
Outputs:
- correlation: float32 [16, 2, 16, 32, 1024], P('gz', None, 'row', 'col')
The draws below stay inside these ranges and needn't reach their ends.
All inputs are finite; a program needn't handle non-finite values.
Results may differ from the reference program's by a relative error of at most 0.011.
Values may be sent and summed in bfloat16 or wider, within the bound.
No kernel may reach another device: no remote copies, remote signals or barrier semaphores. Data moves between devices by JAX's collectives and lax.ppermute only.
A program may use at most 64 MiB of HBM per device.

```python
import math
import jax
import jax.numpy as jnp
from jax import lax

PATCH = 160
STRIDE = 128
OFF = 32
RIM = 16
SECTIONS = 16
HEIGHT = 2048
WIDTH = 4096


def steps_of(own_key, dims, cuts, least, largest):
    def one(dim, parts):
        heights = jax.random.uniform(jax.random.fold_in(jax.random.fold_in(own_key, 6), dim), (parts,), jnp.float32, least / len(cuts), largest / len(cuts))
        return jnp.repeat(jnp.exp(heights), dims[dim] // parts).reshape((-1,) + (1,) * (len(dims) - dim - 1))

    gain = one(*cuts[0])
    for cut in cuts[1:]:
        gain = gain * one(*cut)
    return gain


def bell_draw(stream_key, shape, deviation, reach, pieces=(), kind=jnp.bfloat16):
    values = jax.random.normal(stream_key, shape, jnp.float32) * deviation
    if len(pieces) > 0:
        values = steps_of(stream_key, shape, pieces, -0.22, 0.18) * values
    return jnp.clip(values, min=-reach, max=reach).astype(kind)


def setup_inputs(seed: int = 0) -> dict:
    seeds = jax.random.split(jax.random.key(seed), 2)
    sections = bell_draw(seeds[0], (SECTIONS, HEIGHT, WIDTH), 1.0, 6.0, ((0, 8), (1, 4), (2, 8)))
    return {"sections": sections}


full_turn = 2.0 * math.pi

def dft_tables():
    positions = jnp.arange(PATCH, dtype=jnp.int32)
    angles = (positions[:, None] * positions[None, :] % PATCH).astype(jnp.float32) * (full_turn / PATCH)
    cosine_table = jnp.cos(angles)
    sine_table = jnp.sin(angles)
    forward_cat = jnp.concatenate([cosine_table, -sine_table], axis=1).astype(jnp.bfloat16)
    row_mix = jnp.concatenate([jnp.concatenate([cosine_table, sine_table], axis=1), jnp.concatenate([-sine_table, cosine_table], axis=1)], axis=0).astype(jnp.bfloat16)
    shifts = jnp.arange(OFF, dtype=jnp.int32) - OFF // 2
    offset_angles = (positions[:, None] * shifts[None, :] % PATCH).astype(jnp.float32) * (full_turn / PATCH)
    offset_cos = jnp.cos(offset_angles)
    offset_sin = jnp.sin(offset_angles)
    inverse_cat = jnp.concatenate([jnp.concatenate([offset_cos, offset_sin], axis=1), jnp.concatenate([-offset_sin, offset_cos], axis=1)], axis=0).astype(jnp.bfloat16)
    inverse_rows = jnp.concatenate([offset_cos, -offset_sin], axis=0).astype(jnp.bfloat16)
    return (forward_cat, row_mix, inverse_cat, inverse_rows)

def extract(padded_image):
    rows_patch = HEIGHT // STRIDE
    cols_patch = WIDTH // STRIDE
    row_ids = (STRIDE * jnp.arange(rows_patch, dtype=jnp.int32)[:, None] + jnp.arange(PATCH, dtype=jnp.int32)[None, :]).reshape(-1)
    col_ids = (STRIDE * jnp.arange(cols_patch, dtype=jnp.int32)[:, None] + jnp.arange(PATCH, dtype=jnp.int32)[None, :]).reshape(-1)
    picked = jnp.take(padded_image, row_ids, axis=0)
    picked = jnp.take(picked, col_ids, axis=1)
    picked = picked.reshape(rows_patch, PATCH, cols_patch, PATCH).transpose(0, 2, 1, 3)
    return picked.reshape(rows_patch * cols_patch, PATCH, PATCH)

def normalize(patches):
    values = patches.astype(jnp.float32)
    centered = values - lax.optimization_barrier(jnp.mean(values, axis=(-2, -1), keepdims=True))
    inverse_norm = lax.rsqrt(lax.optimization_barrier(jnp.mean(centered * centered, axis=(-2, -1), keepdims=True)) + 1e-05)
    return (centered * inverse_norm).astype(jnp.bfloat16)

def spectrum(normed, tables):
    forward_cat, row_mix, inverse_cat, inverse_rows = tables
    first = jnp.einsum('...mn,nl->...ml', normed.astype(jnp.float32), forward_cat.astype(jnp.float32)).astype(jnp.bfloat16)
    stacked = jnp.concatenate([first[..., :PATCH], first[..., PATCH:]], axis=-2)
    return jnp.einsum('km,...ml->...kl', row_mix.astype(jnp.float32), stacked.astype(jnp.float32)).astype(jnp.bfloat16)

def correlate(left_spec, right_spec, tables):
    forward_cat, row_mix, inverse_cat, inverse_rows = tables
    left_real = left_spec[..., :PATCH, :].astype(jnp.float32)
    left_imag = left_spec[..., PATCH:, :].astype(jnp.float32)
    right_real = right_spec[..., :PATCH, :].astype(jnp.float32)
    right_imag = right_spec[..., PATCH:, :].astype(jnp.float32)
    cross_real = left_real * right_real + left_imag * right_imag
    cross_imag = left_imag * right_real - left_real * right_imag
    cross = jnp.concatenate([cross_real, cross_imag], axis=-1).astype(jnp.bfloat16)
    half_inverse = jnp.einsum('...kl,lv->...kv', cross.astype(jnp.float32), inverse_cat.astype(jnp.float32)).astype(jnp.bfloat16)
    stacked = jnp.concatenate([half_inverse[..., :OFF], half_inverse[..., OFF:]], axis=-2)
    result = jnp.einsum('ku,...kv->...uv', inverse_rows.astype(jnp.float32), stacked.astype(jnp.float32)) * (1.0 / PATCH ** 3)
    return result.reshape(result.shape[:-2] + (OFF * OFF,))

def reference(sections):
    tables = dft_tables()
    padded = jnp.pad(sections, ((0, 0), (RIM, RIM), (RIM, RIM)))
    patch_count = HEIGHT // STRIDE * (WIDTH // STRIDE)
    empty = jnp.zeros((patch_count, 2 * PATCH, PATCH), jnp.bfloat16)

    def advance(carry, section_image):
        nearer, farther = carry
        current = spectrum(normalize(extract(section_image)), tables)
        result = jnp.stack([correlate(current, nearer, tables), correlate(current, farther, tables)], axis=0)
        return ((current, nearer), result)
    final_carry, results = lax.scan(advance, (empty, empty), padded[::-1])
    return results[::-1].reshape(SECTIONS, 2, HEIGHT // STRIDE, WIDTH // STRIDE, OFF * OFF)
```

```python
import functools
import math

import jax
import jax.numpy as jnp
import numpy as np
from jax import lax
from jax.experimental import pallas as pl
from jax.experimental.pallas import tpu as pltpu
from jax.sharding import PartitionSpec as P

PATCH = 160
STRIDE = 128
OFF = 32
RIM = 16
HALF = PATCH // 2
AXES = ("gz", "row", "col")


def tables():
    turn = 2.0 * math.pi / PATCH
    bf = lambda a: np.asarray(a, np.float32).astype(jnp.bfloat16)
    q = np.full(256, -1)
    q[:128] = np.arange(128) + RIM
    q[128 : 128 + RIM] = np.arange(RIM) + 128 + RIM
    q[256 - RIM :] = np.arange(RIM)
    l = np.arange(HALF + 1)
    ang = (q[:, None] * l[None, :] % PATCH) * turn
    live = (q >= 0)[:, None]
    columns = np.zeros((256, 256))
    columns[:, : HALF + 1] = np.where(live, np.cos(ang), 0.0)
    columns[:, 128 : 128 + HALF + 1] = np.where(live, -np.sin(ang), 0.0)
    k = np.arange(HALF)
    m = np.arange(PATCH)
    ang = (k[:, None] * m[None, :] % PATCH) * turn
    sines = np.sin(ang)
    sines[0] = np.where(m % 2 == 0, 1.0, -1.0)
    rows = np.concatenate([np.cos(ang), sines], axis=0)
    place = np.arange(OFF)
    u = (place % 8) * 4 + place // 8
    ang = ((u - OFF // 2)[:, None] * k[None, :] % PATCH) * turn
    sines = np.sin(ang)
    sines[:, 0] = np.where(u % 2 == 0, 1.0, -1.0)
    back_rows = np.concatenate([np.cos(ang), sines], axis=1)
    v = np.arange(OFF) - OFF // 2
    ang = (l[:, None] * v[None, :] % PATCH) * turn
    weight = np.where((l == 0) | (l == HALF), 1.0, 2.0)[:, None]
    one = np.zeros((256, OFF))
    one[: HALF + 1] = np.cos(ang)
    one[128 : 128 + HALF + 1] = -np.sin(ang)
    one = bf(one).astype(np.float32)
    one[: HALF + 1] *= weight
    one[128 : 128 + HALF + 1] *= weight
    back_columns = np.zeros((4, 256, 128))
    for s in range(4):
        back_columns[s, :, s * OFF : (s + 1) * OFF] = one
    return bf(columns), bf(rows), bf(back_rows), bf(back_columns.reshape(1024, 128))


def spectra_of(blocks, rim, columns, rows, live, which):
    lane = lax.broadcasted_iota(jnp.int32, (PATCH, 128), 1)
    head = lane < RIM
    tail = lane >= 128 - RIM
    side_lanes = head | tail
    top = lax.broadcasted_iota(jnp.int32, (HALF, 128), 0) == 0
    normed = []
    for j in which:
        before = blocks[j - 1] if j > 0 else rim
        behind = blocks[j + 1] if j < 3 else rim
        main = blocks[j]
        side = jnp.where(head, behind, jnp.where(tail, before, 0.0))
        mean = jnp.sum(main + side, keepdims=True) * (1.0 / PATCH**2)
        main = main - mean
        side = jnp.where(side_lanes, side - mean, 0.0)
        variance = jnp.sum(main * main + side * side, keepdims=True) * (1.0 / PATCH**2)
        scale = lax.rsqrt(variance + 1e-05)
        if live is not None:
            scale = scale * live
        normed.append(
            jnp.concatenate([(main * scale).astype(jnp.bfloat16), (side * scale).astype(jnp.bfloat16)], axis=1)
        )
    first = jnp.dot(
        jnp.concatenate(normed, axis=0), columns, preferred_element_type=jnp.float32
    ).astype(jnp.bfloat16)
    result = []
    for n in range(len(which)):
        mixed = jnp.dot(rows, first[PATCH * n : PATCH * (n + 1)], preferred_element_type=jnp.float32)
        cos_real, cos_imag = mixed[:HALF, :128], mixed[:HALF, 128:]
        sin_real, sin_imag = mixed[HALF:, :128], mixed[HALF:, 128:]
        plus = [
            jnp.where(top, cos_real, cos_real + sin_imag),
            jnp.where(top, cos_imag, cos_imag - sin_real),
        ]
        minus = [
            jnp.where(top, sin_real, cos_real - sin_imag),
            jnp.where(top, sin_imag, cos_imag + sin_real),
        ]
        real = jnp.concatenate([plus[0], minus[0]], axis=0)
        imag = jnp.concatenate([plus[1], minus[1]], axis=0)
        result.append(jnp.concatenate([real, imag], axis=1).astype(jnp.bfloat16))
    return result


def half_back(left, right, back_rows):
    top = lax.broadcasted_iota(jnp.int32, (HALF, 128), 0) == 0
    left = left.astype(jnp.float32)
    right = right.astype(jnp.float32)
    lr, li, rr, ri = left[:, :128], left[:, 128:], right[:, :128], right[:, 128:]
    real = lr * rr + li * ri
    imag = li * rr - lr * ri
    pr, mr, p_i, mi = real[:HALF], real[HALF:], imag[:HALF], imag[HALF:]
    even = [jnp.where(top, pr, pr + mr), jnp.where(top, p_i, p_i + mi)]
    odd = [jnp.where(top, mr, mi - p_i), jnp.where(top, mi, pr - mr)]
    real = jnp.concatenate([even[0], odd[0]], axis=0)
    imag = jnp.concatenate([even[1], odd[1]], axis=0)
    both = jnp.concatenate([real, imag], axis=1).astype(jnp.bfloat16)
    return jnp.dot(back_rows, both, preferred_element_type=jnp.float32)


def kernel(fresh, kept, pairs, earlier, keep, *refs):
    refs = list(refs)
    live_ref = refs.pop(0)
    padded_ref, rims_ref = refs.pop(0), refs.pop(0)
    kept_ref = refs.pop(0) if kept else None
    earlier_refs = [refs.pop(0) for _ in range(len(earlier))]
    columns_ref, rows_ref, back_rows_ref, back_columns_ref = [refs.pop(0) for _ in range(4)]
    out_ref = refs.pop(0)
    spectra_ref = refs.pop(0) if keep else None
    rim_scr, line_scr = refs
    i = pl.program_id(0)
    tall = rims_ref.shape[-1]

    @pl.when(i == 0)
    def _():
        for s in range(fresh):
            both = rims_ref[s].astype(jnp.float32)
            wide = jnp.concatenate(
                [both[RIM:], jnp.zeros((128 - 2 * RIM, tall), jnp.float32), both[:RIM]], axis=0
            )
            rim_scr[s] = wide.T

    live = live_ref[0] if live_ref is not None else None
    start = pl.multiple_of(i * STRIDE, STRIDE)
    columns, rows = columns_ref[...], rows_ref[...]
    back_rows, back_columns = back_rows_ref[...], back_columns_ref[...]
    spectra = {}
    for s in range(fresh):
        blocks = [
            padded_ref[s, pl.ds(start, PATCH), 128 * b : 128 * (b + 1)].astype(jnp.float32)
            for b in range(4)
        ]
        rim = rim_scr[s, pl.ds(start, PATCH), :]
        spectra[kept + s] = spectra_of(blocks, rim, columns, rows, live, range(4))
        if keep:
            for j in range(4):
                spectra_ref[s, 0, j] = spectra[kept + s][j]
    pieces = []
    for a, b in pairs:
        for j in range(4):
            left = kept_ref[a, 0, j] if a < kept else spectra[a][j]
            right = kept_ref[b, 0, j] if b < kept else spectra[b][j]
            halves = half_back(left, right, back_rows)
            pieces.append(jnp.concatenate([halves[8 * s : 8 * (s + 1)] for s in range(4)], axis=1))
    lines = jnp.concatenate(pieces, axis=0).astype(jnp.bfloat16)
    line_scr[...] = jnp.dot(lines, back_columns, preferred_element_type=jnp.float32) * (
        1.0 / PATCH**3
    )
    base = 0
    for ref in earlier_refs:
        for n in range(ref.shape[0]):
            out_ref[base] = ref[n]
            base += 1
    for n in range(len(pairs)):
        for b in range(8):
            out_ref[base + n, 0, :, 128 * b : 128 * (b + 1)] = line_scr[pl.ds(32 * n + b, 4, stride=8), :]


def stage(padded, rims, kept, pairs, earlier, keep, live, consts):
    fresh = padded.shape[0]
    side = (padded.shape[1] - 2 * RIM) // STRIDE
    held = 0 if kept is None else kept.shape[0]
    whole = lambda a: pl.BlockSpec(a.shape, lambda i: (0,) * a.ndim)
    operands, specs = [live, padded, rims], [
        pl.BlockSpec(memory_space=pltpu.SMEM),
        whole(padded),
        whole(rims),
    ]
    if held:
        operands.append(kept)
        specs.append(pl.BlockSpec((held, 1, 4, PATCH, 256), lambda i: (0, i, 0, 0, 0)))
    for e in earlier:
        operands.append(e)
        specs.append(pl.BlockSpec((e.shape[0], 1, 4, 1024), lambda i: (0, i, 0, 0)))
    for c in consts:
        operands.append(c)
        specs.append(whole(c))
    total = len(pairs) + sum(e.shape[0] for e in earlier)
    out_shape = [jax.ShapeDtypeStruct((total, side, 4, 1024), jnp.float32)]
    out_specs = [pl.BlockSpec((total, 1, 4, 1024), lambda i: (0, i, 0, 0))]
    if keep:
        out_shape.append(jax.ShapeDtypeStruct((fresh, side, 4, PATCH, 256), jnp.bfloat16))
        out_specs.append(pl.BlockSpec((fresh, 1, 4, PATCH, 256), lambda i: (0, i, 0, 0, 0)))
    flops = 2 * side * 4 * (fresh * (PATCH * 65536 + PATCH**2 * 256) + len(pairs) * 64 * PATCH * 256)
    return pl.pallas_call(
        functools.partial(kernel, fresh, held, pairs, earlier, keep),
        grid=(side,),
        in_specs=specs,
        out_specs=out_specs,
        out_shape=out_shape,
        scratch_shapes=[
            pltpu.VMEM((fresh, rims.shape[-1], 128), jnp.float32),
            pltpu.VMEM((32 * len(pairs), 128), jnp.float32),
        ],
        compiler_params=pltpu.CompilerParams(vmem_limit_bytes=40 * 1024 * 1024),
        cost_estimate=pl.CostEstimate(flops=4 * flops, bytes_accessed=padded.size * 2, transcendentals=0),
    )(*operands)


def ring(value, axis, steps):
    count = lax.axis_size(axis)
    return lax.ppermute(value, axis, [(n, (n + steps) % count) for n in range(count)])


def shards(sections):
    consts = [jnp.asarray(t) for t in tables()]
    height = sections.shape[1]
    row, col, gz = lax.axis_index("row"), lax.axis_index("col"), lax.axis_index("gz")
    rows, cols, blocks = lax.axis_size("row"), lax.axis_size("col"), lax.axis_size("gz")
    above = jnp.where(row > 0, ring(sections[:, height - RIM :], "row", 1), 0)
    below = jnp.where(row < rows - 1, ring(sections[:, :RIM], "row", -1), 0)
    padded = jnp.concatenate([above, sections, below], axis=1)
    arriving = [ring(padded[n : n + 1], "gz", -1) for n in range(2)]
    tall = height + 2 * RIM
    fill = ((0, 0), (0, 0), (0, -tall % 128))
    left = jnp.where(col > 0, ring(jnp.swapaxes(padded[:, :, -RIM:], 1, 2), "col", 1), 0)
    right = jnp.where(col < cols - 1, ring(jnp.swapaxes(padded[:, :, :RIM], 1, 2), "col", -1), 0)
    rims = jnp.pad(jnp.concatenate([left, right], axis=1), fill)
    far_rims = ring(rims, "gz", -1)
    one = jnp.ones((1,), jnp.float32)
    live = (gz < blocks - 1).astype(jnp.float32).reshape(1)
    near, spectra = stage(padded, rims, None, [(0, 1)], [], True, one, consts)
    middle, = stage(arriving[0], far_rims[:1], spectra, [(0, 2), (1, 2)], [], False, live, consts)
    result, = stage(arriving[1], far_rims[1:], spectra, [(1, 2)], [near, middle], False, live, consts)
    return result.reshape(2, 2, result.shape[1], 4, OFF * OFF)


def solution(mesh):
    return jax.shard_map(
        shards,
        mesh=mesh,
        in_specs=(P("gz", "row", "col"),),
        out_specs=P("gz", None, "row", "col", None),
        check_vma=False,
    )
```

```python
import functools
import math

import jax
import jax.numpy as jnp
import numpy as np
from jax import lax
from jax.experimental import pallas as pl
from jax.experimental.pallas import tpu as pltpu
from jax.sharding import PartitionSpec as P

PATCH = 160
STRIDE = 128
OFF = 32
CUT = 272
STAGE_COST = 30
EDGES_COST = 10_000_000_000
RIM = 16
HALF = PATCH // 2
AXES = ("gz", "row", "col")


def tables():
    turn = 2.0 * math.pi / PATCH
    bf = lambda a: np.asarray(a, np.float32).astype(jnp.bfloat16)
    q = np.full(256, -1)
    q[:128] = np.arange(128) + RIM
    q[128 : 128 + RIM] = np.arange(RIM) + 128 + RIM
    q[256 - RIM :] = np.arange(RIM)
    l = np.arange(HALF + 1)
    ang = (q[:, None] * l[None, :] % PATCH) * turn
    live = (q >= 0)[:, None]
    columns = np.zeros((256, 256))
    columns[:, : HALF + 1] = np.where(live, np.cos(ang), 0.0)
    columns[:, 128 : 128 + HALF + 1] = np.where(live, -np.sin(ang), 0.0)
    k = np.arange(HALF)
    m = np.arange(PATCH)
    ang = (k[:, None] * m[None, :] % PATCH) * turn
    sines = np.sin(ang)
    sines[0] = np.where(m % 2 == 0, 1.0, -1.0)
    rows = np.concatenate([np.cos(ang), sines], axis=0)
    place = np.arange(OFF)
    u = (place % 8) * 4 + place // 8
    ang = ((u - OFF // 2)[:, None] * k[None, :] % PATCH) * turn
    sines = np.sin(ang)
    sines[:, 0] = np.where(u % 2 == 0, 1.0, -1.0)
    back_rows = np.concatenate([np.cos(ang), sines], axis=1)
    v = np.arange(OFF) - OFF // 2
    ang = (l[:, None] * v[None, :] % PATCH) * turn
    weight = np.where((l == 0) | (l == HALF), 1.0, 2.0)[:, None]
    one = np.zeros((256, OFF))
    one[: HALF + 1] = np.cos(ang)
    one[128 : 128 + HALF + 1] = -np.sin(ang)
    one = bf(one).astype(np.float32)
    one[: HALF + 1] *= weight
    one[128 : 128 + HALF + 1] *= weight
    back_columns = np.zeros((4, 256, 128))
    for s in range(4):
        back_columns[s, :, s * OFF : (s + 1) * OFF] = one
    return bf(columns), bf(rows), bf(back_rows), bf(back_columns.reshape(1024, 128))


def total(a):
    a = jnp.sum(a.reshape(PATCH // 8, 8, 128), axis=0)
    return jnp.sum(jnp.sum(a, axis=1, keepdims=True), axis=0, keepdims=True)


def with_top(special, rest):
    top = lax.broadcasted_iota(jnp.int32, (8, 128), 0) == 0
    return jnp.concatenate([jnp.where(top, special[:8], rest[:8]), rest[8:]], axis=0)


def spectra_of(blocks, rim, columns, rows, live):
    lane = lax.broadcasted_iota(jnp.int32, (PATCH, 128), 1)
    head = lane < RIM
    tail = lane >= 128 - RIM
    side_lanes = head | tail
    result = []
    for j in range(4):
        before = blocks[j - 1] if j > 0 else rim
        behind = blocks[j + 1] if j < 3 else rim
        main = blocks[j]
        side = jnp.where(head, behind, jnp.where(tail, before, 0.0))
        mean = total(main + side) * (1.0 / PATCH**2)
        main = main - mean
        side = jnp.where(side_lanes, side - mean, 0.0)
        scale = lax.rsqrt(total(main * main + side * side) * (1.0 / PATCH**2) + 1e-05)
        if live is not None:
            scale = scale * live
        normed = jnp.concatenate(
            [(main * scale).astype(jnp.bfloat16), (side * scale).astype(jnp.bfloat16)], axis=1
        )
        first = jnp.dot(normed, columns, preferred_element_type=jnp.float32).astype(jnp.bfloat16)
        mixed = jnp.dot(rows, first, preferred_element_type=jnp.float32)
        cos_real, cos_imag = mixed[:HALF, :128], mixed[:HALF, 128:]
        sin_real, sin_imag = mixed[HALF:, :128], mixed[HALF:, 128:]
        plus = [with_top(cos_real, cos_real + sin_imag), with_top(cos_imag, cos_imag - sin_real)]
        minus = [with_top(sin_real, cos_real - sin_imag), with_top(sin_imag, cos_imag + sin_real)]
        both = [jnp.concatenate(plus, axis=1), jnp.concatenate(minus, axis=1)]
        result.append(jnp.concatenate(both, axis=0).astype(jnp.bfloat16))
    return result


def half_back(left, right, back_rows):
    left = left.astype(jnp.float32)
    right = right.astype(jnp.float32)
    lr, li, rr, ri = left[:, :128], left[:, 128:], right[:, :128], right[:, 128:]
    real = lr * rr + li * ri
    imag = li * rr - lr * ri
    pr, mr, p_i, mi = real[:HALF], real[HALF:], imag[:HALF], imag[HALF:]
    even = [with_top(pr, pr + mr), with_top(p_i, p_i + mi)]
    odd = [with_top(mr, mi - p_i), with_top(mi, pr - mr)]
    both = [jnp.concatenate(even, axis=1), jnp.concatenate(odd, axis=1)]
    both = jnp.concatenate(both, axis=0).astype(jnp.bfloat16)
    return jnp.dot(back_rows, both, preferred_element_type=jnp.float32)


def edges_kernel(flags_ref, first_ref, last_ref, above_ref, below_ref, low_ref, high_ref):
    up = (flags_ref[0] > 0).astype(jnp.float32)
    down = (flags_ref[1] > 0).astype(jnp.float32)
    for s in range(2):
        for block, ref, take in ((0, low_ref, 0), (1, high_ref, 128 - RIM)):
            tile = (first_ref, last_ref)[block][s].astype(jnp.float32)
            lanes = slice(0, 128) if block == 0 else slice(384, 512)
            top = above_ref[s, :, lanes].astype(jnp.float32) * up
            bottom = below_ref[s, :, lanes].astype(jnp.float32) * down
            tall = jnp.concatenate([top, tile, bottom, jnp.zeros((96, 128), jnp.float32)], axis=0)
            ref[s] = tall.T[take : take + RIM].astype(jnp.bfloat16)


def rims_kernel(flags_ref, above_ref, below_ref, left_ref, right_ref, rims_ref):
    for n, ref in enumerate((above_ref, below_ref, left_ref, right_ref)):
        keep = (flags_ref[n] > 0).astype(jnp.float32)
        part = (ref[...].astype(jnp.float32) * keep).astype(jnp.bfloat16)
        if n < 2:
            rims_ref[:, RIM * n : RIM * (n + 1), :512] = part
            rims_ref[:, RIM * n : RIM * (n + 1), 512:] = jnp.zeros((2, RIM, 128), jnp.bfloat16)
        else:
            rims_ref[:, RIM * n : RIM * (n + 1), :] = part


def kernel(plan, *refs):
    fresh, kept, pairs, at, keep, masked, cuts, span = plan
    refs = list(refs)
    flags_ref = refs.pop(0)
    tile_refs = [refs.pop(0) for _ in cuts]
    rims_ref = refs.pop(0)
    kept_ref = refs.pop(0) if kept else None
    if at:
        refs.pop(0)
    columns_ref, rows_ref, back_rows_ref, back_columns_ref = [refs.pop(0) for _ in range(4)]
    out_ref = refs.pop(0)
    spectra_ref = refs.pop(0)
    rim_scr, half_scr, line_scr, wide_scr, sem = refs
    live = (flags_ref[4] > 0).astype(jnp.float32) if masked else None
    columns, rows = columns_ref[...], rows_ref[...]
    back_rows, back_columns = back_rows_ref[...], back_columns_ref[...]
    for n, s in enumerate(fresh):
        both = rims_ref[s, 2 * RIM :].astype(jnp.float32)
        gap = jnp.zeros((128 - 2 * RIM, both.shape[1]), jnp.float32)
        rim_scr[n] = jnp.concatenate([both[RIM:], gap, both[:RIM]], axis=0).T
    for i in range(*span):
        for n, s in enumerate(fresh):
            blocks = []
            low, high = STRIDE * i - RIM, STRIDE * (i + 1) + RIM
            for b in range(4):
                lanes = slice(128 * b, 128 * (b + 1))
                parts = []
                if low < 0:
                    parts.append(rims_ref[s, :RIM, lanes])
                for ref, start in zip(tile_refs, cuts):
                    begin, end = max(low, start), min(high, start + ref.shape[1])
                    if begin < end:
                        parts.append(ref[n, begin - start : end - start, lanes])
                if high > 512:
                    parts.append(rims_ref[s, RIM : 2 * RIM, lanes])
                parts = [part.astype(jnp.float32) for part in parts]
                blocks.append(jnp.concatenate(parts, axis=0) if len(parts) > 1 else parts[0])
            rim = rim_scr[n, STRIDE * i : STRIDE * i + PATCH, :]
            for j, one in enumerate(spectra_of(blocks, rim, columns, rows, live)):
                spectra_ref[n, i - span[0], j] = one
    tall = 32 * (span[1] - span[0])
    for i in range(*span):
        for n, (a, b) in enumerate(pairs):
            for j in range(4):
                left = kept_ref[a, i, j] if a < kept else spectra_ref[a - kept, i - span[0], j]
                right = kept_ref[b, i, j] if b < kept else spectra_ref[b - kept, i - span[0], j]
                halves = half_back(left, right, back_rows)
                place = tall * n + 32 * (i - span[0]) + 8 * j
                for t in range(4):
                    half_scr[place : place + 8, 256 * t : 256 * (t + 1)] = halves[8 * t : 8 * (t + 1)]
    line_scr[...] = jnp.dot(
        half_scr[...].astype(jnp.bfloat16), back_columns, preferred_element_type=jnp.float32
    ) * (1.0 / PATCH**3)
    for n in range(len(pairs)):
        for i in range(span[1] - span[0]):
            for b in range(8):
                wide_scr[n, i, :, 128 * b : 128 * (b + 1)] = line_scr[
                    pl.ds(tall * n + 32 * i + b, 4, stride=8), :
                ]
    copy = pltpu.make_async_copy(
        wide_scr, out_ref.at[pl.ds(at, len(pairs)), pl.ds(span[0], span[1] - span[0])], sem
    )
    copy.start()
    copy.wait()


IN_VMEM = pl.BlockSpec(memory_space=pltpu.VMEM)
IN_SMEM = pl.BlockSpec(memory_space=pltpu.SMEM)
ANYWHERE = pl.BlockSpec(memory_space=pl.ANY)
PARAMS = pltpu.CompilerParams(vmem_limit_bytes=24 * 1024 * 1024)


def stage(flags, tiles, rims, kept, earlier, consts, fresh, pairs, at, keep, masked, span=(0, 4)):
    held = 0 if kept is None else kept.shape[0]
    operands, aliases = [flags, *tiles.values(), rims], {}
    specs = [IN_SMEM] + [IN_VMEM] * (len(tiles) + 1)
    if held:
        operands.append(kept)
        specs.append(IN_VMEM)
    if earlier is not None:
        aliases[len(operands)] = 0
        operands.append(earlier)
        specs.append(ANYWHERE)
    operands += consts
    specs += [IN_VMEM] * len(consts)
    out_shape = [jax.ShapeDtypeStruct((4, 4, 4, 1024), jnp.float32)]
    out_specs = [ANYWHERE]
    if keep:
        out_shape.append(jax.ShapeDtypeStruct((len(fresh), 4, 4, PATCH, 256), jnp.bfloat16))
        out_specs.append(IN_VMEM)
    height = span[1] - span[0]
    flops = 2 * 4 * height * (len(fresh) * (PATCH * 65536 + PATCH**2 * 256) + len(pairs) * 64 * PATCH * 256)
    return pl.pallas_call(
        functools.partial(kernel, (fresh, held, pairs, at, keep, masked, tuple(tiles), span)),
        in_specs=specs,
        out_specs=out_specs,
        out_shape=out_shape,
        input_output_aliases=aliases,
        scratch_shapes=([] if keep else [pltpu.VMEM((len(fresh), height, 4, PATCH, 256), jnp.bfloat16)])
        + [
            pltpu.VMEM((len(fresh), rims.shape[-1], 128), jnp.float32),
            pltpu.VMEM((32 * height * len(pairs), 1024), jnp.float32),
            pltpu.VMEM((32 * height * len(pairs), 128), jnp.float32),
            pltpu.VMEM((len(pairs), height, 4, 1024), jnp.float32),
            pltpu.SemaphoreType.DMA,
        ],
        compiler_params=PARAMS,
        cost_estimate=pl.CostEstimate(flops=STAGE_COST * flops, bytes_accessed=1 << 20, transcendentals=0),
    )(*operands)


def ring(value, axis, steps):
    count = lax.axis_size(axis)
    return lax.ppermute(value, axis, [(n, (n + steps) % count) for n in range(count)])


def shards(sections):
    consts = [jnp.asarray(t) for t in tables()]
    height, width = sections.shape[1:]
    row, col, gz = lax.axis_index("row"), lax.axis_index("col"), lax.axis_index("gz")
    rows, cols, depth = lax.axis_size("row"), lax.axis_size("col"), lax.axis_size("gz")
    flags = jnp.stack([row > 0, row < rows - 1, col > 0, col < cols - 1, gz < depth - 1]).astype(jnp.int32)
    above = ring(sections[:, height - RIM :], "row", 1)
    below = ring(sections[:, :RIM], "row", -1)
    first = ring(sections[:1], "gz", -1)
    upper = ring(sections[1:, :CUT], "gz", -1)
    blocks = lax.optimization_barrier((sections[:, :, :128], sections[:, :, width - 128 :]))

    def around(operands):
        flags, first_block, last_block, above, below = operands
        edge = jax.ShapeDtypeStruct((2, RIM, 640), jnp.bfloat16)
        low, high = pl.pallas_call(
            edges_kernel,
            in_specs=[IN_SMEM] + [IN_VMEM] * 4,
            out_specs=[IN_VMEM, IN_VMEM],
            out_shape=[edge, edge],
            compiler_params=PARAMS,
            cost_estimate=pl.CostEstimate(flops=EDGES_COST, bytes_accessed=1 << 20, transcendentals=0),
        )(flags, first_block, last_block, above, below)
        left = ring(high, "col", 1)
        right = ring(low, "col", -1)
        rims = pl.pallas_call(
            rims_kernel,
            in_specs=[IN_SMEM] + [IN_VMEM] * 4,
            out_specs=IN_VMEM,
            out_shape=jax.ShapeDtypeStruct((2, 4 * RIM, 640), jnp.bfloat16),
            compiler_params=PARAMS,
        )(flags, above, below, left, right)
        return rims

    rims = lax.cond(
        jnp.sum(flags) < 99,
        around,
        lambda operands: jnp.zeros((2, 4 * RIM, 640), jnp.bfloat16),
        (flags, *blocks, above, below),
    )
    far = ring(rims, "gz", -1)
    result, spectra = stage(flags, {0: sections}, rims, None, None, consts, (0, 1), [(0, 1)], 0, True, False)
    later, spectra = lax.optimization_barrier((sections, spectra))
    lower = ring(later[1:, CUT:], "gz", -1)
    result, = stage(flags, {0: first}, far, spectra, result, consts, (0,), [(0, 2), (1, 2)], 1, False, True)
    result, = stage(
        flags, {0: upper}, far, spectra, result, consts, (1,), [(1, 2)], 3, False, True, (0, 2)
    )
    both = {0: upper, CUT: lower}
    result, = stage(flags, both, far, spectra, result, consts, (1,), [(1, 2)], 3, False, True, (2, 4))
    return result.reshape(2, 2, 4, 4, OFF * OFF)


def solution(mesh):
    return jax.shard_map(
        shards,
        mesh=mesh,
        in_specs=(P("gz", "row", "col"),),
        out_specs=P("gz", None, "row", "col", None),
        check_vma=False,
    )
```

```python
import functools
import math

import jax
import jax.numpy as jnp
import numpy as np
from jax import lax
from jax.experimental import pallas as pl
from jax.experimental.pallas import tpu as pltpu
from jax.sharding import PartitionSpec as P

PATCH = 160
STRIDE = 128
OFF = 32
CUT = 144
CUTS = (CUT, 512)
SPANS = ((1, 4),)
RIM = 16
HALF = PATCH // 2
AXES = ("gz", "row", "col")


def tables():
    turn = 2.0 * math.pi / PATCH
    bf = lambda a: np.asarray(a, np.float32).astype(jnp.bfloat16)
    q = np.full(256, -1)
    q[:128] = np.arange(128) + RIM
    q[128 : 128 + RIM] = np.arange(RIM) + 128 + RIM
    q[256 - RIM :] = np.arange(RIM)
    l = np.arange(HALF + 1)
    ang = (q[:, None] * l[None, :] % PATCH) * turn
    live = (q >= 0)[:, None]
    columns = np.zeros((256, 256))
    columns[:, : HALF + 1] = np.where(live, np.cos(ang), 0.0)
    columns[:, 128 : 128 + HALF + 1] = np.where(live, -np.sin(ang), 0.0)
    k = np.arange(HALF)
    m = np.arange(PATCH)
    ang = (k[:, None] * m[None, :] % PATCH) * turn
    sines = np.sin(ang)
    sines[0] = np.where(m % 2 == 0, 1.0, -1.0)
    rows = np.concatenate([np.cos(ang), sines], axis=0)
    place = np.arange(OFF)
    u = (place % 8) * 4 + place // 8
    ang = ((u - OFF // 2)[:, None] * k[None, :] % PATCH) * turn
    sines = np.sin(ang)
    sines[:, 0] = np.where(u % 2 == 0, 1.0, -1.0)
    back_rows = np.concatenate([np.cos(ang), sines], axis=1)
    v = np.arange(OFF) - OFF // 2
    ang = (l[:, None] * v[None, :] % PATCH) * turn
    weight = np.where((l == 0) | (l == HALF), 1.0, 2.0)[:, None]
    one = np.zeros((256, OFF))
    one[: HALF + 1] = np.cos(ang)
    one[128 : 128 + HALF + 1] = -np.sin(ang)
    one = bf(one).astype(np.float32)
    one[: HALF + 1] *= weight
    one[128 : 128 + HALF + 1] *= weight
    back_columns = np.zeros((4, 256, 128))
    for s in range(4):
        back_columns[s, :, s * OFF : (s + 1) * OFF] = one
    return bf(columns), bf(rows), bf(back_rows), bf(back_columns.reshape(1024, 128))


def total(a):
    a = jnp.sum(a.reshape(PATCH // 8, 8, 128), axis=0)
    return jnp.sum(jnp.sum(a, axis=1, keepdims=True), axis=0, keepdims=True)


def with_top(special, rest):
    top = lax.broadcasted_iota(jnp.int32, (8, 128), 0) == 0
    return jnp.concatenate([jnp.where(top, special[:8], rest[:8]), rest[8:]], axis=0)


def spectra_of(blocks, rim, columns, rows, live, which):
    lane = lax.broadcasted_iota(jnp.int32, (PATCH, 128), 1)
    head = lane < RIM
    tail = lane >= 128 - RIM
    side_lanes = head | tail
    result = []
    for j in which:
        before = blocks[j - 1] if j > 0 else rim
        behind = blocks[j + 1] if j < 3 else rim
        main = blocks[j]
        side = jnp.where(head, behind, jnp.where(tail, before, 0.0))
        mean = total(main + side) * (1.0 / PATCH**2)
        main = main - mean
        side = jnp.where(side_lanes, side - mean, 0.0)
        scale = lax.rsqrt(total(main * main + side * side) * (1.0 / PATCH**2) + 1e-05)
        if live is not None:
            scale = scale * live
        normed = jnp.concatenate(
            [(main * scale).astype(jnp.bfloat16), (side * scale).astype(jnp.bfloat16)], axis=1
        )
        first = jnp.dot(normed, columns, preferred_element_type=jnp.float32).astype(jnp.bfloat16)
        mixed = jnp.dot(rows, first, preferred_element_type=jnp.float32)
        cos_real, cos_imag = mixed[:HALF, :128], mixed[:HALF, 128:]
        sin_real, sin_imag = mixed[HALF:, :128], mixed[HALF:, 128:]
        plus = [with_top(cos_real, cos_real + sin_imag), with_top(cos_imag, cos_imag - sin_real)]
        minus = [with_top(sin_real, cos_real - sin_imag), with_top(sin_imag, cos_imag + sin_real)]
        both = [jnp.concatenate(plus, axis=1), jnp.concatenate(minus, axis=1)]
        result.append(jnp.concatenate(both, axis=0).astype(jnp.bfloat16))
    return result


def half_back(left, right, back_rows):
    left = left.astype(jnp.float32)
    right = right.astype(jnp.float32)
    lr, li, rr, ri = left[:, :128], left[:, 128:], right[:, :128], right[:, 128:]
    real = lr * rr + li * ri
    imag = li * rr - lr * ri
    pr, mr, p_i, mi = real[:HALF], real[HALF:], imag[:HALF], imag[HALF:]
    even = [with_top(pr, pr + mr), with_top(p_i, p_i + mi)]
    odd = [with_top(mr, mi - p_i), with_top(mi, pr - mr)]
    both = [jnp.concatenate(even, axis=1), jnp.concatenate(odd, axis=1)]
    both = jnp.concatenate(both, axis=0).astype(jnp.bfloat16)
    return jnp.dot(back_rows, both, preferred_element_type=jnp.float32)


def cut_kernel(parts, tile_ref, *refs):
    sems = refs[-1]
    copies = [
        pltpu.make_async_copy(tile_ref.at[pl.ds(*deep), pl.ds(*tall)], ref, sems.at[n])
        for n, ((deep, tall), ref) in enumerate(zip(parts, refs))
    ]
    for copy in copies:
        copy.start()
    for copy in copies:
        copy.wait()


def edges_kernel(flags_ref, tile_ref, above_ref, below_ref, low_ref, high_ref):
    up = (flags_ref[0] > 0).astype(jnp.float32)
    down = (flags_ref[1] > 0).astype(jnp.float32)
    for s in range(2):
        for block, ref, take in ((0, low_ref, 0), (1, high_ref, 128 - RIM)):
            lanes = slice(0, 128) if block == 0 else slice(384, 512)
            tile = tile_ref[s, :, lanes].astype(jnp.float32)
            top = above_ref[s, :, lanes].astype(jnp.float32) * up
            bottom = below_ref[s, :, lanes].astype(jnp.float32) * down
            tall = jnp.concatenate([top, tile, bottom, jnp.zeros((96, 128), jnp.float32)], axis=0)
            ref[s] = tall.T[take : take + RIM].astype(jnp.bfloat16)


def rims_kernel(flags_ref, above_ref, below_ref, left_ref, right_ref, rims_ref):
    for n, ref in enumerate((above_ref, below_ref, left_ref, right_ref)):
        keep = (flags_ref[n] > 0).astype(jnp.float32)
        part = (ref[...].astype(jnp.float32) * keep).astype(jnp.bfloat16)
        if n < 2:
            rims_ref[:, RIM * n : RIM * (n + 1), :512] = part
            rims_ref[:, RIM * n : RIM * (n + 1), 512:] = jnp.zeros((2, RIM, 128), jnp.bfloat16)
        else:
            rims_ref[:, RIM * n : RIM * (n + 1), :] = part


def window(parts, i, b):
    low, high = STRIDE * i - RIM, STRIDE * (i + 1) + RIM
    pieces = []
    for read, start, stop in parts:
        begin, end = max(low, start), min(high, stop)
        if begin < end:
            pieces.append(read(slice(begin - start, end - start), slice(128 * b, 128 * (b + 1))))
    return jnp.concatenate(pieces, axis=0) if len(pieces) > 1 else pieces[0]


def reader(ref, s, first=0, factor=None):
    def read(lines, lanes):
        value = ref[s, first + lines.start : first + lines.stop, lanes].astype(jnp.float32)
        return value if factor is None else value * factor

    return read


def inner_kernel(flags_ref, tile_ref, above_ref, below_ref, columns_ref, rows_ref, inner_ref):
    up = (flags_ref[0] > 0).astype(jnp.float32)
    down = (flags_ref[1] > 0).astype(jnp.float32)
    columns, rows = columns_ref[...], rows_ref[...]
    for i in range(4):
        for s in range(2):
            parts = [
                (reader(above_ref, s, 0, up), -RIM, 0),
                (reader(tile_ref, s), 0, 512),
                (reader(below_ref, s, 0, down), 512, 512 + RIM),
            ]
            blocks = [window(parts, i, b) for b in range(4)]
            for n, one in enumerate(spectra_of(blocks, None, columns, rows, None, (1, 2))):
                inner_ref[s, i, n] = one


def side_blocks(rims_ref, s):
    both = rims_ref[s, 2 * RIM :].astype(jnp.float32)
    gap = jnp.zeros((128 - 2 * RIM, both.shape[1]), jnp.float32)
    return jnp.concatenate([both[RIM:], gap, both[:RIM]], axis=0).T


def outer_kernel(flags_ref, tile_ref, rims_ref, inner_ref, columns_ref, rows_ref, outer_ref, rim_scr):
    columns, rows = columns_ref[...], rows_ref[...]
    for s in range(2):
        rim_scr[s] = side_blocks(rims_ref, s)
    for i in range(4):
        for s in range(2):
            parts = [
                (reader(rims_ref, s), -RIM, 0),
                (reader(tile_ref, s), 0, 512),
                (reader(rims_ref, s, RIM), 512, 512 + RIM),
            ]
            blocks = [window(parts, i, b) for b in range(4)]
            rim = rim_scr[s, STRIDE * i : STRIDE * i + PATCH, :]
            for n, one in enumerate(spectra_of(blocks, rim, columns, rows, None, (0, 3))):
                outer_ref[s, i, n] = one


def kernel(plan, *refs):
    fresh, pairs, at, cuts, span = plan
    refs = list(refs)
    flags_ref = refs.pop(0)
    tile_refs = [refs.pop(0) for _ in cuts]
    rims_ref, inner_ref, outer_ref = refs.pop(0), refs.pop(0), refs.pop(0)
    if at:
        refs.pop(0)
    columns_ref, rows_ref, back_rows_ref, back_columns_ref = [refs.pop(0) for _ in range(4)]
    out_ref, fresh_ref, rim_scr, half_scr, line_scr, wide_scr, sem = refs
    live = (flags_ref[4] > 0).astype(jnp.float32)
    columns, rows = columns_ref[...], rows_ref[...]
    back_rows, back_columns = back_rows_ref[...], back_columns_ref[...]
    for n, s in enumerate(fresh):
        rim_scr[n] = side_blocks(rims_ref, s)
    for i in range(*span):
        for n, s in enumerate(fresh):
            parts = [(reader(rims_ref, s), -RIM, 0)]
            for ref, start in zip(tile_refs, cuts):
                parts.append((reader(ref, n), start, start + ref.shape[1]))
            parts.append((reader(rims_ref, s, RIM), 512, 512 + RIM))
            blocks = [window(parts, i, b) for b in range(4)]
            rim = rim_scr[n, STRIDE * i : STRIDE * i + PATCH, :]
            for m, one in enumerate(spectra_of(blocks, rim, columns, rows, live, range(4))):
                fresh_ref[n, i - span[0], m] = one

    def spectrum(section, i, j):
        if section >= 2:
            return fresh_ref[section - 2, i - span[0], j]
        return inner_ref[section, i, j - 1] if j in (1, 2) else outer_ref[section, i, j // 3]

    tall = 32 * (span[1] - span[0])
    for i in range(*span):
        for n, (a, b) in enumerate(pairs):
            for j in range(4):
                halves = half_back(spectrum(a, i, j), spectrum(b, i, j), back_rows)
                place = tall * n + 32 * (i - span[0]) + 8 * j
                for t in range(4):
                    half_scr[place : place + 8, 256 * t : 256 * (t + 1)] = halves[8 * t : 8 * (t + 1)]
    line_scr[...] = jnp.dot(
        half_scr[...].astype(jnp.bfloat16), back_columns, preferred_element_type=jnp.float32
    ) * (1.0 / PATCH**3)
    for n in range(len(pairs)):
        for i in range(span[1] - span[0]):
            for b in range(8):
                wide_scr[n, i, :, 128 * b : 128 * (b + 1)] = line_scr[
                    pl.ds(tall * n + 32 * i + b, 4, stride=8), :
                ]
    copy = pltpu.make_async_copy(
        wide_scr, out_ref.at[pl.ds(at, len(pairs)), pl.ds(span[0], span[1] - span[0])], sem
    )
    copy.start()
    copy.wait()


IN_VMEM = pl.BlockSpec(memory_space=pltpu.VMEM)
IN_SMEM = pl.BlockSpec(memory_space=pltpu.SMEM)
ANYWHERE = pl.BlockSpec(memory_space=pl.ANY)
PARAMS = pltpu.CompilerParams(vmem_limit_bytes=9 * 1024 * 1024)


def cost(flops):
    return pl.CostEstimate(flops=flops, bytes_accessed=1 << 20, transcendentals=0)


def stage(flags, tiles, rims, inner, outer, earlier, consts, fresh, pairs, at, span=(0, 4)):
    height = span[1] - span[0]
    operands, aliases = [flags, *tiles.values(), rims, inner, outer], {}
    specs = [IN_SMEM] + [IN_VMEM] * (len(operands) - 1)
    if at:
        aliases[len(operands)] = 0
        operands.append(earlier)
        specs.append(ANYWHERE)
    operands += consts
    specs += [IN_VMEM] * len(consts)
    return pl.pallas_call(
        functools.partial(kernel, (fresh, pairs, at, tuple(tiles), span)),
        in_specs=specs,
        out_specs=ANYWHERE,
        out_shape=jax.ShapeDtypeStruct((4, 4, 4, 1024), jnp.float32),
        input_output_aliases=aliases,
        scratch_shapes=[
            pltpu.VMEM((len(fresh), height, 4, PATCH, 256), jnp.bfloat16),
            pltpu.VMEM((len(fresh), 640, 128), jnp.float32),
            pltpu.VMEM((32 * height * len(pairs), 1024), jnp.float32),
            pltpu.VMEM((32 * height * len(pairs), 128), jnp.float32),
            pltpu.VMEM((len(pairs), height, 4, 1024), jnp.float32),
            pltpu.SemaphoreType.DMA,
        ],
        compiler_params=PARAMS,
        cost_estimate=cost(60_000_000_000),
    )(*operands)


def cut(sections, parts):
    return pl.pallas_call(
        functools.partial(cut_kernel, parts),
        in_specs=[pl.BlockSpec(memory_space=pltpu.HBM)],
        out_specs=[IN_VMEM] * len(parts),
        out_shape=[
            jax.ShapeDtypeStruct((deep[1], tall[1], sections.shape[2]), jnp.bfloat16) for deep, tall in parts
        ],
        scratch_shapes=[pltpu.SemaphoreType.DMA((len(parts),))],
        compiler_params=PARAMS,
    )(sections)


def ring(value, axis, steps):
    count = lax.axis_size(axis)
    return lax.ppermute(value, axis, [(n, (n + steps) % count) for n in range(count)])


def shards(sections):
    consts = [jnp.asarray(t) for t in tables()]
    height, width = sections.shape[1:]
    row, col, gz = lax.axis_index("row"), lax.axis_index("col"), lax.axis_index("gz")
    rows, cols, depth = lax.axis_size("row"), lax.axis_size("col"), lax.axis_size("gz")
    flags = jnp.stack([row > 0, row < rows - 1, col > 0, col < cols - 1, gz < depth - 1]).astype(jnp.int32)
    bf = lambda *shape: jax.ShapeDtypeStruct(shape, jnp.bfloat16)
    top, bottom = cut(sections, [((0, 2), (0, RIM)), ((0, 2), (height - RIM, RIM))])
    first, upper = cut(sections, [((0, 1), (0, height)), ((1, 1), (0, CUT))])
    above = ring(bottom, "row", 1)
    below = ring(top, "row", -1)
    first = ring(first, "gz", -1)
    upper = ring(upper, "gz", -1)

    def around(operands):
        flags, tile, above, below = operands
        low, high = pl.pallas_call(
            edges_kernel,
            in_specs=[IN_SMEM] + [IN_VMEM] * 3,
            out_specs=[IN_VMEM, IN_VMEM],
            out_shape=[bf(2, RIM, 640), bf(2, RIM, 640)],
            compiler_params=PARAMS,
        )(flags, tile, above, below)
        left = ring(high, "col", 1)
        right = ring(low, "col", -1)
        inner = pl.pallas_call(
            inner_kernel,
            in_specs=[IN_SMEM] + [IN_VMEM] * 5,
            out_specs=IN_VMEM,
            out_shape=bf(2, 4, 2, PATCH, 256),
            compiler_params=PARAMS,
            cost_estimate=cost(10_000_000_000),
        )(flags, tile, above, below, consts[0], consts[1])
        rims = pl.pallas_call(
            rims_kernel,
            in_specs=[IN_SMEM] + [IN_VMEM] * 4,
            out_specs=IN_VMEM,
            out_shape=bf(2, 4 * RIM, 640),
            compiler_params=PARAMS,
        )(flags, above, below, left, right)
        return rims, inner

    def nothing(operands):
        return jnp.zeros((2, 4 * RIM, 640), jnp.bfloat16), jnp.zeros((2, 4, 2, PATCH, 256), jnp.bfloat16)

    rims, inner = lax.cond(
        row + col + gz < 99, around, nothing, (flags, sections, above, below)
    )
    far = ring(rims, "gz", -1)
    outer = pl.pallas_call(
        outer_kernel,
        in_specs=[IN_SMEM] + [IN_VMEM] * 5,
        out_specs=IN_VMEM,
        out_shape=bf(2, 4, 2, PATCH, 256),
        scratch_shapes=[pltpu.VMEM((2, 640, 128), jnp.float32)],
        compiler_params=PARAMS,
        cost_estimate=cost(60_000_000_000),
    )(flags, sections, rims, inner, consts[0], consts[1])
    later, outer = lax.optimization_barrier((sections, outer))
    lower = cut(later, [((1, 1), (a, b - a)) for a, b in zip(CUTS[:-1], CUTS[1:])])
    lower = [ring(part, "gz", -1) for part in lower]
    pairs = [(0, 1), (0, 2), (1, 2)]
    result = stage(flags, {0: first}, far, inner, outer, None, consts, (0,), pairs, 0)
    parts = {0: upper}
    spans = list(SPANS)
    if spans[0][0]:
        result = stage(flags, parts, far, inner, outer, result, consts, (1,), [(1, 2)], 3, (0, spans[0][0]))
    for start, part, span in zip(CUTS, lower, spans):
        parts = {**parts, start: part}
        result = stage(flags, parts, far, inner, outer, result, consts, (1,), [(1, 2)], 3, span)
    return result.reshape(2, 2, 4, 4, OFF * OFF)


def solution(mesh):
    return jax.shard_map(
        shards,
        mesh=mesh,
        in_specs=(P("gz", "row", "col"),),
        out_specs=P("gz", None, "row", "col", None),
        check_vma=False,
    )
```

```python
import functools
import math

import jax
import jax.numpy as jnp
import numpy as np
from jax import lax
from jax.experimental import pallas as pl
from jax.experimental.pallas import tpu as pltpu
from jax.sharding import PartitionSpec as P

PATCH = 160
STRIDE = 128
OFF = 32
CUT = 144
CUTS = (CUT, 512)
SPANS = ((1, 4),)
RIM = 16
HALF = PATCH // 2
AXES = ("gz", "row", "col")


def tables():
    turn = 2.0 * math.pi / PATCH
    bf = lambda a: np.asarray(a, np.float32).astype(jnp.bfloat16)
    q = np.full(256, -1)
    q[:128] = np.arange(128) + RIM
    q[128 : 128 + RIM] = np.arange(RIM) + 128 + RIM
    q[256 - RIM :] = np.arange(RIM)
    l = np.arange(HALF + 1)
    ang = (q[:, None] * l[None, :] % PATCH) * turn
    live = (q >= 0)[:, None]
    columns = np.zeros((256, 256))
    columns[:, : HALF + 1] = np.where(live, np.cos(ang), 0.0)
    columns[:, 128 : 128 + HALF + 1] = np.where(live, -np.sin(ang), 0.0)
    k = np.arange(HALF)
    m = np.arange(PATCH)
    ang = (k[:, None] * m[None, :] % PATCH) * turn
    sines = np.sin(ang)
    sines[0] = np.where(m % 2 == 0, 1.0, -1.0)
    rows = np.concatenate([np.cos(ang), sines], axis=0)
    place = np.arange(OFF)
    u = (place % 8) * 4 + place // 8
    ang = ((u - OFF // 2)[:, None] * k[None, :] % PATCH) * turn
    sines = np.sin(ang)
    sines[:, 0] = np.where(u % 2 == 0, 1.0, -1.0)
    back_rows = np.concatenate([np.cos(ang), sines], axis=1)
    v = np.arange(OFF) - OFF // 2
    ang = (l[:, None] * v[None, :] % PATCH) * turn
    weight = np.where((l == 0) | (l == HALF), 1.0, 2.0)[:, None]
    one = np.zeros((256, OFF))
    one[: HALF + 1] = np.cos(ang)
    one[128 : 128 + HALF + 1] = -np.sin(ang)
    one = bf(one).astype(np.float32)
    one[: HALF + 1] *= weight
    one[128 : 128 + HALF + 1] *= weight
    back_columns = np.zeros((4, 256, 128))
    for s in range(4):
        back_columns[s, :, s * OFF : (s + 1) * OFF] = one
    return bf(columns), bf(rows), bf(back_rows), bf(back_columns.reshape(1024, 128))


def total(a):
    a = jnp.sum(a.reshape(PATCH // 8, 8, 128), axis=0)
    return jnp.sum(jnp.sum(a, axis=1, keepdims=True), axis=0, keepdims=True)


def with_top(special, rest):
    top = lax.broadcasted_iota(jnp.int32, (8, 128), 0) == 0
    return jnp.concatenate([jnp.where(top, special[:8], rest[:8]), rest[8:]], axis=0)


def spectra_of(blocks, rim, columns, rows, live, which):
    lane = lax.broadcasted_iota(jnp.int32, (PATCH, 128), 1)
    head = lane < RIM
    tail = lane >= 128 - RIM
    side_lanes = head | tail
    result = []
    for j in which:
        before = blocks[j - 1] if j > 0 else rim
        behind = blocks[j + 1] if j < 3 else rim
        main = blocks[j]
        side = jnp.where(head, behind, jnp.where(tail, before, 0.0))
        mean = total(main + side) * (1.0 / PATCH**2)
        main = main - mean
        side = jnp.where(side_lanes, side - mean, 0.0)
        scale = lax.rsqrt(total(main * main + side * side) * (1.0 / PATCH**2) + 1e-05)
        if live is not None:
            scale = scale * live
        normed = jnp.concatenate(
            [(main * scale).astype(jnp.bfloat16), (side * scale).astype(jnp.bfloat16)], axis=1
        )
        first = jnp.dot(normed, columns, preferred_element_type=jnp.float32).astype(jnp.bfloat16)
        mixed = jnp.dot(rows, first, preferred_element_type=jnp.float32)
        cos_real, cos_imag = mixed[:HALF, :128], mixed[:HALF, 128:]
        sin_real, sin_imag = mixed[HALF:, :128], mixed[HALF:, 128:]
        plus = [with_top(cos_real, cos_real + sin_imag), with_top(cos_imag, cos_imag - sin_real)]
        minus = [with_top(sin_real, cos_real - sin_imag), with_top(sin_imag, cos_imag + sin_real)]
        both = [jnp.concatenate(plus, axis=1), jnp.concatenate(minus, axis=1)]
        result.append(jnp.concatenate(both, axis=0).astype(jnp.bfloat16))
    return result


def half_back(left, right, back_rows):
    left = left.astype(jnp.float32)
    right = right.astype(jnp.float32)
    lr, li, rr, ri = left[:, :128], left[:, 128:], right[:, :128], right[:, 128:]
    real = lr * rr + li * ri
    imag = li * rr - lr * ri
    pr, mr, p_i, mi = real[:HALF], real[HALF:], imag[:HALF], imag[HALF:]
    even = [with_top(pr, pr + mr), with_top(p_i, p_i + mi)]
    odd = [with_top(mr, mi - p_i), with_top(mi, pr - mr)]
    both = [jnp.concatenate(even, axis=1), jnp.concatenate(odd, axis=1)]
    both = jnp.concatenate(both, axis=0).astype(jnp.bfloat16)
    return jnp.dot(back_rows, both, preferred_element_type=jnp.float32)


def inside(axis, ahead):
    place = lax.axis_index(axis)
    there = place < lax.axis_size(axis) - 1 if ahead else place > 0
    return there.astype(jnp.float32)


def cut_kernel(parts, tile_ref, *refs):
    sems = refs[-1]
    copies = [
        pltpu.make_async_copy(tile_ref.at[pl.ds(*deep), pl.ds(*tall)], ref, sems.at[n])
        for n, ((deep, tall), ref) in enumerate(zip(parts, refs))
    ]
    for copy in copies:
        copy.start()
    for copy in copies:
        copy.wait()


def edges_kernel(tile_ref, above_ref, below_ref, low_ref, high_ref):
    up = inside("row", False)
    down = inside("row", True)
    for s in range(2):
        for block, ref, take in ((0, low_ref, 0), (1, high_ref, 128 - RIM)):
            lanes = slice(0, 128) if block == 0 else slice(384, 512)
            tile = tile_ref[s, :, lanes].astype(jnp.float32)
            top = above_ref[s, :, lanes].astype(jnp.float32) * up
            bottom = below_ref[s, :, lanes].astype(jnp.float32) * down
            tall = jnp.concatenate([top, tile, bottom, jnp.zeros((96, 128), jnp.float32)], axis=0)
            ref[s] = tall.T[take : take + RIM].astype(jnp.bfloat16)


def rims_kernel(above_ref, below_ref, left_ref, right_ref, rims_ref):
    for n, ref in enumerate((above_ref, below_ref, left_ref, right_ref)):
        keep = inside("row" if n < 2 else "col", n % 2 == 1)
        part = (ref[...].astype(jnp.float32) * keep).astype(jnp.bfloat16)
        if n < 2:
            rims_ref[:, RIM * n : RIM * (n + 1), :512] = part
            rims_ref[:, RIM * n : RIM * (n + 1), 512:] = jnp.zeros((2, RIM, 128), jnp.bfloat16)
        else:
            rims_ref[:, RIM * n : RIM * (n + 1), :] = part


def window(parts, i, b):
    low, high = STRIDE * i - RIM, STRIDE * (i + 1) + RIM
    pieces = []
    for read, start, stop in parts:
        begin, end = max(low, start), min(high, stop)
        if begin < end:
            pieces.append(read(slice(begin - start, end - start), slice(128 * b, 128 * (b + 1))))
    return jnp.concatenate(pieces, axis=0) if len(pieces) > 1 else pieces[0]


def reader(ref, s, first=0, factor=None):
    def read(lines, lanes):
        value = ref[s, first + lines.start : first + lines.stop, lanes].astype(jnp.float32)
        return value if factor is None else value * factor

    return read


def inner_kernel(tile_ref, above_ref, below_ref, columns_ref, rows_ref, inner_ref):
    up = inside("row", False)
    down = inside("row", True)
    columns, rows = columns_ref[...], rows_ref[...]
    for i in range(4):
        for s in range(2):
            parts = [
                (reader(above_ref, s, 0, up), -RIM, 0),
                (reader(tile_ref, s), 0, 512),
                (reader(below_ref, s, 0, down), 512, 512 + RIM),
            ]
            blocks = [window(parts, i, b) for b in range(4)]
            for n, one in enumerate(spectra_of(blocks, None, columns, rows, None, (1, 2))):
                inner_ref[s, i, n] = one


def side_blocks(rims_ref, s):
    both = rims_ref[s, 2 * RIM :].astype(jnp.float32)
    gap = jnp.zeros((128 - 2 * RIM, both.shape[1]), jnp.float32)
    return jnp.concatenate([both[RIM:], gap, both[:RIM]], axis=0).T


def outer_kernel(tile_ref, rims_ref, inner_ref, columns_ref, rows_ref, outer_ref, rim_scr):
    columns, rows = columns_ref[...], rows_ref[...]
    for s in range(2):
        rim_scr[s] = side_blocks(rims_ref, s)
    for i in range(4):
        for s in range(2):
            parts = [
                (reader(rims_ref, s), -RIM, 0),
                (reader(tile_ref, s), 0, 512),
                (reader(rims_ref, s, RIM), 512, 512 + RIM),
            ]
            blocks = [window(parts, i, b) for b in range(4)]
            rim = rim_scr[s, STRIDE * i : STRIDE * i + PATCH, :]
            for n, one in enumerate(spectra_of(blocks, rim, columns, rows, None, (0, 3))):
                outer_ref[s, i, n] = one


def kernel(plan, *refs):
    fresh, pairs, at, cuts, span = plan
    refs = list(refs)
    tile_refs = [refs.pop(0) for _ in cuts]
    rims_ref, inner_ref, outer_ref = refs.pop(0), refs.pop(0), refs.pop(0)
    if at:
        given_ref = refs.pop(0)
        refs.pop(0)
    columns_ref, rows_ref, back_rows_ref, back_columns_ref = [refs.pop(0) for _ in range(4)]
    out_ref = refs.pop(0)
    side_ref = None if at else refs.pop(0)
    fresh_ref, rim_scr, half_scr, line_scr, wide_scr, sem = refs
    live = inside("gz", True)
    columns, rows = columns_ref[...], rows_ref[...]
    back_rows, back_columns = back_rows_ref[...], back_columns_ref[...]
    if not at:
        rim_scr[0] = side_blocks(rims_ref, 0)
        side_ref[...] = side_blocks(rims_ref, 1)
    for i in range(*span):
        for n, s in enumerate(fresh):
            parts = [(reader(rims_ref, s), -RIM, 0)]
            for ref, start in zip(tile_refs, cuts):
                parts.append((reader(ref, n), start, start + ref.shape[1]))
            parts.append((reader(rims_ref, s, RIM), 512, 512 + RIM))
            blocks = [window(parts, i, b) for b in range(4)]
            lines = slice(STRIDE * i, STRIDE * i + PATCH)
            rim = given_ref[lines, :] if at else rim_scr[n, lines, :]
            for m, one in enumerate(spectra_of(blocks, rim, columns, rows, live, range(4))):
                fresh_ref[n, i - span[0], m] = one

    def spectrum(section, i, j):
        if section >= 2:
            return fresh_ref[section - 2, i - span[0], j]
        return inner_ref[section, i, j - 1] if j in (1, 2) else outer_ref[section, i, j // 3]

    tall = 32 * (span[1] - span[0])
    for i in range(*span):
        for n, (a, b) in enumerate(pairs):
            for j in range(4):
                halves = half_back(spectrum(a, i, j), spectrum(b, i, j), back_rows)
                place = tall * n + 32 * (i - span[0]) + 8 * j
                for t in range(4):
                    half_scr[place : place + 8, 256 * t : 256 * (t + 1)] = halves[8 * t : 8 * (t + 1)]
    line_scr[...] = jnp.dot(
        half_scr[...].astype(jnp.bfloat16), back_columns, preferred_element_type=jnp.float32
    ) * (1.0 / PATCH**3)
    for n in range(len(pairs)):
        for i in range(span[1] - span[0]):
            for b in range(8):
                wide_scr[n, i, :, 128 * b : 128 * (b + 1)] = line_scr[
                    pl.ds(tall * n + 32 * i + b, 4, stride=8), :
                ]
    copy = pltpu.make_async_copy(
        wide_scr, out_ref.at[pl.ds(at, len(pairs)), pl.ds(span[0], span[1] - span[0])], sem
    )
    copy.start()
    copy.wait()


IN_VMEM = pl.BlockSpec(memory_space=pltpu.VMEM)
ANYWHERE = pl.BlockSpec(memory_space=pl.ANY)
PARAMS = pltpu.CompilerParams(vmem_limit_bytes=9 * 1024 * 1024)


def cost(flops):
    return pl.CostEstimate(flops=flops, bytes_accessed=1 << 20, transcendentals=0)


def stage(tiles, rims, inner, outer, earlier, consts, fresh, pairs, at, span=(0, 4)):
    height = span[1] - span[0]
    operands, aliases = [*tiles.values(), rims, inner, outer], {}
    specs = [IN_VMEM] * len(operands)
    if at:
        aliases[len(operands) + 1] = 0
        operands += earlier
        specs += [IN_VMEM, ANYWHERE]
    operands += consts
    specs += [IN_VMEM] * len(consts)
    return pl.pallas_call(
        functools.partial(kernel, (fresh, pairs, at, tuple(tiles), span)),
        in_specs=specs,
        out_specs=[ANYWHERE] if at else [ANYWHERE, IN_VMEM],
        out_shape=[jax.ShapeDtypeStruct((4, 4, 4, 1024), jnp.float32)]
        + ([] if at else [jax.ShapeDtypeStruct((640, 128), jnp.float32)]),
        input_output_aliases=aliases,
        scratch_shapes=[
            pltpu.VMEM((len(fresh), height, 4, PATCH, 256), jnp.bfloat16),
            pltpu.VMEM((len(fresh), 640, 128), jnp.float32),
            pltpu.VMEM((32 * height * len(pairs), 1024), jnp.float32),
            pltpu.VMEM((32 * height * len(pairs), 128), jnp.float32),
            pltpu.VMEM((len(pairs), height, 4, 1024), jnp.float32),
            pltpu.SemaphoreType.DMA,
        ],
        compiler_params=PARAMS,
        cost_estimate=cost(60_000_000_000),
    )(*operands)


def cut(sections, parts):
    return pl.pallas_call(
        functools.partial(cut_kernel, parts),
        in_specs=[pl.BlockSpec(memory_space=pltpu.HBM)],
        out_specs=[IN_VMEM] * len(parts),
        out_shape=[
            jax.ShapeDtypeStruct((deep[1], tall[1], sections.shape[2]), jnp.bfloat16) for deep, tall in parts
        ],
        scratch_shapes=[pltpu.SemaphoreType.DMA((len(parts),))],
        compiler_params=PARAMS,
    )(sections)


def ring(value, axis, steps):
    count = lax.axis_size(axis)
    return lax.ppermute(value, axis, [(n, (n + steps) % count) for n in range(count)])


def shards(sections):
    consts = [jnp.asarray(t) for t in tables()]
    height, width = sections.shape[1:]
    row, col, gz = lax.axis_index("row"), lax.axis_index("col"), lax.axis_index("gz")
    bf = lambda *shape: jax.ShapeDtypeStruct(shape, jnp.bfloat16)
    top, bottom = cut(sections, [((0, 2), (0, RIM)), ((0, 2), (height - RIM, RIM))])
    first, upper = cut(sections, [((0, 1), (0, height)), ((1, 1), (0, CUT))])
    above = ring(bottom, "row", 1)
    below = ring(top, "row", -1)
    first = ring(first, "gz", -1)
    upper = ring(upper, "gz", -1)

    def around(operands):
        tile, above, below = operands
        low, high = pl.pallas_call(
            edges_kernel,
            in_specs=[IN_VMEM] * 3,
            out_specs=[IN_VMEM, IN_VMEM],
            out_shape=[bf(2, RIM, 640), bf(2, RIM, 640)],
            compiler_params=PARAMS,
        )(tile, above, below)
        left = ring(high, "col", 1)
        right = ring(low, "col", -1)
        inner = pl.pallas_call(
            inner_kernel,
            in_specs=[IN_VMEM] * 5,
            out_specs=IN_VMEM,
            out_shape=bf(2, 4, 2, PATCH, 256),
            compiler_params=PARAMS,
            cost_estimate=cost(10_000_000_000),
        )(tile, above, below, consts[0], consts[1])
        rims = pl.pallas_call(
            rims_kernel,
            in_specs=[IN_VMEM] * 4,
            out_specs=IN_VMEM,
            out_shape=bf(2, 4 * RIM, 640),
            compiler_params=PARAMS,
        )(above, below, left, right)
        return rims, inner

    def nothing(operands):
        return jnp.zeros((2, 4 * RIM, 640), jnp.bfloat16), jnp.zeros((2, 4, 2, PATCH, 256), jnp.bfloat16)

    rims, inner = lax.cond(
        row + col + gz < 99, around, nothing, (sections, above, below)
    )
    far = ring(rims, "gz", -1)
    outer = pl.pallas_call(
        outer_kernel,
        in_specs=[IN_VMEM] * 5,
        out_specs=IN_VMEM,
        out_shape=bf(2, 4, 2, PATCH, 256),
        scratch_shapes=[pltpu.VMEM((2, 640, 128), jnp.float32)],
        compiler_params=PARAMS,
        cost_estimate=cost(60_000_000_000),
    )(sections, rims, inner, consts[0], consts[1])
    later, outer = lax.optimization_barrier((sections, outer))
    lower = cut(later, [((1, 1), (a, b - a)) for a, b in zip(CUTS[:-1], CUTS[1:])])
    lower = [ring(part, "gz", -1) for part in lower]
    pairs = [(0, 1), (0, 2), (1, 2)]
    result, side = stage({0: first}, far, inner, outer, None, consts, (0,), pairs, 0)
    parts = {0: upper}
    spans = list(SPANS)
    if spans[0][0]:
        result, = stage(parts, far, inner, outer, (side, result), consts, (1,), [(1, 2)], 3, (0, spans[0][0]))
    for start, part, span in zip(CUTS, lower, spans):
        parts = {**parts, start: part}
        result, = stage(parts, far, inner, outer, (side, result), consts, (1,), [(1, 2)], 3, span)
    return result.reshape(2, 2, 4, 4, OFF * OFF)


def solution(mesh):
    return jax.shard_map(
        shards,
        mesh=mesh,
        in_specs=(P("gz", "row", "col"),),
        out_specs=P("gz", None, "row", "col", None),
        check_vma=False,
    )
```

```python
import functools
import math

import jax
import jax.numpy as jnp
import numpy as np
from jax import lax
from jax.experimental import pallas as pl
from jax.experimental.pallas import tpu as pltpu
from jax.sharding import PartitionSpec as P

PATCH = 160
STRIDE = 128
OFF = 32
CUT = 144
CUTS = (CUT, 512)
SPANS = ((1, 4),)
RIM = 16
HALF = PATCH // 2
AXES = ("gz", "row", "col")


def tables():
    turn = 2.0 * math.pi / PATCH
    bf = lambda a: np.asarray(a, np.float32).astype(jnp.bfloat16)
    q = np.full(256, -1)
    q[:128] = np.arange(128) + RIM
    q[128 : 128 + RIM] = np.arange(RIM) + 128 + RIM
    q[256 - RIM :] = np.arange(RIM)
    l = np.arange(HALF + 1)
    ang = (q[:, None] * l[None, :] % PATCH) * turn
    live = (q >= 0)[:, None]
    columns = np.zeros((256, 256))
    columns[:, : HALF + 1] = np.where(live, np.cos(ang), 0.0)
    columns[:, 128 : 128 + HALF + 1] = np.where(live, -np.sin(ang), 0.0)
    k = np.arange(HALF)
    m = np.arange(PATCH)
    ang = (k[:, None] * m[None, :] % PATCH) * turn
    sines = np.sin(ang)
    sines[0] = np.where(m % 2 == 0, 1.0, -1.0)
    rows = np.concatenate([np.cos(ang), sines], axis=0)
    place = np.arange(OFF)
    u = (place % 8) * 4 + place // 8
    ang = ((u - OFF // 2)[:, None] * k[None, :] % PATCH) * turn
    sines = np.sin(ang)
    sines[:, 0] = np.where(u % 2 == 0, 1.0, -1.0)
    back_rows = np.concatenate([np.cos(ang), sines], axis=1)
    v = np.arange(OFF) - OFF // 2
    ang = (l[:, None] * v[None, :] % PATCH) * turn
    weight = np.where((l == 0) | (l == HALF), 1.0, 2.0)[:, None]
    one = np.zeros((256, OFF))
    one[: HALF + 1] = np.cos(ang)
    one[128 : 128 + HALF + 1] = -np.sin(ang)
    one = bf(one).astype(np.float32)
    one[: HALF + 1] *= weight
    one[128 : 128 + HALF + 1] *= weight
    back_columns = np.zeros((4, 256, 128))
    for s in range(4):
        back_columns[s, :, s * OFF : (s + 1) * OFF] = one
    return bf(columns), bf(rows), bf(back_rows), bf(back_columns.reshape(1024, 128))


def total(a):
    a = jnp.sum(a.reshape(PATCH // 8, 8, 128), axis=0)
    return jnp.sum(jnp.sum(a, axis=1, keepdims=True), axis=0, keepdims=True)


def with_top(special, rest):
    tile = 32 // special.dtype.itemsize
    top = lax.broadcasted_iota(jnp.int32, (tile, 128), 0) == 0
    return jnp.concatenate([jnp.where(top, special[:tile], rest[:tile]), rest[tile:]], axis=0)


def spectra_of(blocks, rim, columns, rows, live, which):
    lane = lax.broadcasted_iota(jnp.int32, (PATCH, 128), 1)
    head = lane < RIM
    tail = lane >= 128 - RIM
    side_lanes = head | tail
    result = []
    for j in which:
        before = blocks[j - 1] if j > 0 else rim
        behind = blocks[j + 1] if j < 3 else rim
        main = blocks[j]
        side = jnp.where(head, behind, jnp.where(tail, before, 0.0))
        mean = total(main + side) * (1.0 / PATCH**2)
        main = main - mean
        side = jnp.where(side_lanes, side - mean, 0.0)
        scale = lax.rsqrt(total(main * main + side * side) * (1.0 / PATCH**2) + 1e-05)
        if live is not None:
            scale = scale * live
        normed = jnp.concatenate(
            [(main * scale).astype(jnp.bfloat16), (side * scale).astype(jnp.bfloat16)], axis=1
        )
        first = jnp.dot(normed, columns, preferred_element_type=jnp.float32).astype(jnp.bfloat16)
        mixed = jnp.dot(rows, first, preferred_element_type=jnp.float32)
        cos_real, cos_imag = mixed[:HALF, :128], mixed[:HALF, 128:]
        sin_real, sin_imag = mixed[HALF:, :128], mixed[HALF:, 128:]
        plus = [with_top(cos_real, cos_real + sin_imag), with_top(cos_imag, cos_imag - sin_real)]
        minus = [with_top(sin_real, cos_real - sin_imag), with_top(sin_imag, cos_imag + sin_real)]
        both = [jnp.concatenate(plus, axis=1), jnp.concatenate(minus, axis=1)]
        result.append(jnp.concatenate(both, axis=0).astype(jnp.bfloat16))
    return result


def half_back(left, right, back_rows):
    lr, li, rr, ri = left[:, :128], left[:, 128:], right[:, :128], right[:, 128:]
    real = lr * rr + li * ri
    imag = li * rr - lr * ri
    pr, mr, p_i, mi = real[:HALF], real[HALF:], imag[:HALF], imag[HALF:]
    even = [with_top(pr, pr + mr), with_top(p_i, p_i + mi)]
    odd = [with_top(mr, mi - p_i), with_top(mi, pr - mr)]
    both = [jnp.concatenate(even, axis=1), jnp.concatenate(odd, axis=1)]
    both = jnp.concatenate(both, axis=0)
    return jnp.dot(back_rows, both, preferred_element_type=jnp.float32)


def inside(axis, ahead):
    place = lax.axis_index(axis)
    there = place < lax.axis_size(axis) - 1 if ahead else place > 0
    return there.astype(jnp.float32)


def cut_kernel(parts, tile_ref, *refs):
    sems = refs[-1]
    copies = [
        pltpu.make_async_copy(tile_ref.at[pl.ds(*deep), pl.ds(*tall)], ref, sems.at[n])
        for n, ((deep, tall), ref) in enumerate(zip(parts, refs))
    ]
    for copy in copies:
        copy.start()
    for copy in copies:
        copy.wait()


def edges_kernel(tile_ref, above_ref, below_ref, low_ref, high_ref):
    up = inside("row", False)
    down = inside("row", True)
    for s in range(2):
        for block, ref, take in ((0, low_ref, 0), (1, high_ref, 128 - RIM)):
            lanes = slice(0, 128) if block == 0 else slice(384, 512)
            tile = tile_ref[s, :, lanes].astype(jnp.float32)
            top = above_ref[s, :, lanes].astype(jnp.float32) * up
            bottom = below_ref[s, :, lanes].astype(jnp.float32) * down
            tall = jnp.concatenate([top, tile, bottom, jnp.zeros((96, 128), jnp.float32)], axis=0)
            ref[s] = tall.T[take : take + RIM].astype(jnp.bfloat16)


def rims_kernel(above_ref, below_ref, left_ref, right_ref, rims_ref):
    for n, ref in enumerate((above_ref, below_ref, left_ref, right_ref)):
        keep = inside("row" if n < 2 else "col", n % 2 == 1)
        part = (ref[...].astype(jnp.float32) * keep).astype(jnp.bfloat16)
        if n < 2:
            rims_ref[:, RIM * n : RIM * (n + 1), :512] = part
            rims_ref[:, RIM * n : RIM * (n + 1), 512:] = jnp.zeros((2, RIM, 128), jnp.bfloat16)
        else:
            rims_ref[:, RIM * n : RIM * (n + 1), :] = part


def window(parts, i, b):
    low, high = STRIDE * i - RIM, STRIDE * (i + 1) + RIM
    pieces = []
    for read, start, stop in parts:
        begin, end = max(low, start), min(high, stop)
        if begin < end:
            pieces.append(read(slice(begin - start, end - start), slice(128 * b, 128 * (b + 1))))
    return jnp.concatenate(pieces, axis=0) if len(pieces) > 1 else pieces[0]


def reader(ref, s, first=0, factor=None):
    def read(lines, lanes):
        value = ref[s, first + lines.start : first + lines.stop, lanes].astype(jnp.float32)
        return value if factor is None else value * factor

    return read


def inner_kernel(tile_ref, above_ref, below_ref, columns_ref, rows_ref, inner_ref):
    up = inside("row", False)
    down = inside("row", True)
    columns, rows = columns_ref[...], rows_ref[...]
    for i in range(4):
        for s in range(2):
            parts = [
                (reader(above_ref, s, 0, up), -RIM, 0),
                (reader(tile_ref, s), 0, 512),
                (reader(below_ref, s, 0, down), 512, 512 + RIM),
            ]
            blocks = [window(parts, i, b) for b in range(4)]
            for n, one in enumerate(spectra_of(blocks, None, columns, rows, None, (1, 2))):
                inner_ref[s, i, n] = one


def side_blocks(rims_ref, s):
    both = rims_ref[s, 2 * RIM :].astype(jnp.float32)
    gap = jnp.zeros((128 - 2 * RIM, both.shape[1]), jnp.float32)
    return jnp.concatenate([both[RIM:], gap, both[:RIM]], axis=0).T


def outer_kernel(tile_ref, rims_ref, inner_ref, columns_ref, rows_ref, outer_ref, rim_scr):
    columns, rows = columns_ref[...], rows_ref[...]
    for s in range(2):
        rim_scr[s] = side_blocks(rims_ref, s)
    for i in range(4):
        for s in range(2):
            parts = [
                (reader(rims_ref, s), -RIM, 0),
                (reader(tile_ref, s), 0, 512),
                (reader(rims_ref, s, RIM), 512, 512 + RIM),
            ]
            blocks = [window(parts, i, b) for b in range(4)]
            rim = rim_scr[s, STRIDE * i : STRIDE * i + PATCH, :]
            for n, one in enumerate(spectra_of(blocks, rim, columns, rows, None, (0, 3))):
                outer_ref[s, i, n] = one


def kernel(plan, *refs):
    fresh, pairs, at, cuts, span = plan
    refs = list(refs)
    tile_refs = [refs.pop(0) for _ in cuts]
    rims_ref, inner_ref, outer_ref = refs.pop(0), refs.pop(0), refs.pop(0)
    if at:
        given_ref = refs.pop(0)
        refs.pop(0)
    columns_ref, rows_ref, back_rows_ref, back_columns_ref = [refs.pop(0) for _ in range(4)]
    out_ref = refs.pop(0)
    side_ref = None if at else refs.pop(0)
    fresh_ref, rim_scr, half_scr, line_scr, wide_scr, sem = refs
    live = inside("gz", True)
    columns, rows = columns_ref[...], rows_ref[...]
    back_rows, back_columns = back_rows_ref[...], back_columns_ref[...]
    if not at:
        rim_scr[0] = side_blocks(rims_ref, 0)
        side_ref[...] = side_blocks(rims_ref, 1)
    for i in range(*span):
        for n, s in enumerate(fresh):
            parts = [(reader(rims_ref, s), -RIM, 0)]
            for ref, start in zip(tile_refs, cuts):
                parts.append((reader(ref, n), start, start + ref.shape[1]))
            parts.append((reader(rims_ref, s, RIM), 512, 512 + RIM))
            blocks = [window(parts, i, b) for b in range(4)]
            lines = slice(STRIDE * i, STRIDE * i + PATCH)
            rim = given_ref[lines, :] if at else rim_scr[n, lines, :]
            for m, one in enumerate(spectra_of(blocks, rim, columns, rows, live, range(4))):
                fresh_ref[n, i - span[0], m] = one

    def spectrum(section, i, j):
        if section >= 2:
            return fresh_ref[section - 2, i - span[0], j]
        return inner_ref[section, i, j - 1] if j in (1, 2) else outer_ref[section, i, j // 3]

    tall = 32 * (span[1] - span[0])
    for i in range(*span):
        for n, (a, b) in enumerate(pairs):
            for j in range(4):
                halves = half_back(spectrum(a, i, j), spectrum(b, i, j), back_rows)
                place = tall * n + 32 * (i - span[0]) + 8 * j
                for t in range(4):
                    half_scr[place : place + 8, 256 * t : 256 * (t + 1)] = halves[8 * t : 8 * (t + 1)]
    line_scr[...] = jnp.dot(
        half_scr[...].astype(jnp.bfloat16), back_columns, preferred_element_type=jnp.float32
    ) * (1.0 / PATCH**3)
    for n in range(len(pairs)):
        for i in range(span[1] - span[0]):
            for b in range(8):
                wide_scr[n, i, :, 128 * b : 128 * (b + 1)] = line_scr[
                    pl.ds(tall * n + 32 * i + b, 4, stride=8), :
                ]
    copy = pltpu.make_async_copy(
        wide_scr, out_ref.at[pl.ds(at, len(pairs)), pl.ds(span[0], span[1] - span[0])], sem
    )
    copy.start()
    copy.wait()


IN_VMEM = pl.BlockSpec(memory_space=pltpu.VMEM)
ANYWHERE = pl.BlockSpec(memory_space=pl.ANY)
PARAMS = pltpu.CompilerParams(vmem_limit_bytes=9 * 1024 * 1024)


def cost(flops):
    return pl.CostEstimate(flops=flops, bytes_accessed=1 << 20, transcendentals=0)


def stage(tiles, rims, inner, outer, earlier, consts, fresh, pairs, at, span=(0, 4)):
    height = span[1] - span[0]
    operands, aliases = [*tiles.values(), rims, inner, outer], {}
    specs = [IN_VMEM] * len(operands)
    if at:
        aliases[len(operands) + 1] = 0
        operands += earlier
        specs += [IN_VMEM, ANYWHERE]
    operands += consts
    specs += [IN_VMEM] * len(consts)
    return pl.pallas_call(
        functools.partial(kernel, (fresh, pairs, at, tuple(tiles), span)),
        in_specs=specs,
        out_specs=[ANYWHERE] if at else [ANYWHERE, IN_VMEM],
        out_shape=[jax.ShapeDtypeStruct((4, 4, 4, 1024), jnp.float32)]
        + ([] if at else [jax.ShapeDtypeStruct((640, 128), jnp.float32)]),
        input_output_aliases=aliases,
        scratch_shapes=[
            pltpu.VMEM((len(fresh), height, 4, PATCH, 256), jnp.bfloat16),
            pltpu.VMEM((len(fresh), 640, 128), jnp.float32),
            pltpu.VMEM((32 * height * len(pairs), 1024), jnp.float32),
            pltpu.VMEM((32 * height * len(pairs), 128), jnp.float32),
            pltpu.VMEM((len(pairs), height, 4, 1024), jnp.float32),
            pltpu.SemaphoreType.DMA,
        ],
        compiler_params=PARAMS,
        cost_estimate=cost(60_000_000_000),
    )(*operands)


def cut(sections, parts):
    return pl.pallas_call(
        functools.partial(cut_kernel, parts),
        in_specs=[pl.BlockSpec(memory_space=pltpu.HBM)],
        out_specs=[IN_VMEM] * len(parts),
        out_shape=[
            jax.ShapeDtypeStruct((deep[1], tall[1], sections.shape[2]), jnp.bfloat16) for deep, tall in parts
        ],
        scratch_shapes=[pltpu.SemaphoreType.DMA((len(parts),))],
        compiler_params=PARAMS,
    )(sections)


def ring(value, axis, steps):
    count = lax.axis_size(axis)
    return lax.ppermute(value, axis, [(n, (n + steps) % count) for n in range(count)])


def shards(sections):
    consts = [jnp.asarray(t) for t in tables()]
    height, width = sections.shape[1:]
    row, col, gz = lax.axis_index("row"), lax.axis_index("col"), lax.axis_index("gz")
    bf = lambda *shape: jax.ShapeDtypeStruct(shape, jnp.bfloat16)
    top, bottom = cut(sections, [((0, 2), (0, RIM)), ((0, 2), (height - RIM, RIM))])
    first, upper = cut(sections, [((0, 1), (0, height)), ((1, 1), (0, CUT))])
    above = ring(bottom, "row", 1)
    below = ring(top, "row", -1)
    first = ring(first, "gz", -1)
    upper = ring(upper, "gz", -1)

    def around(operands):
        tile, above, below = operands
        low, high = pl.pallas_call(
            edges_kernel,
            in_specs=[IN_VMEM] * 3,
            out_specs=[IN_VMEM, IN_VMEM],
            out_shape=[bf(2, RIM, 640), bf(2, RIM, 640)],
            compiler_params=PARAMS,
        )(tile, above, below)
        left = ring(high, "col", 1)
        right = ring(low, "col", -1)
        inner = pl.pallas_call(
            inner_kernel,
            in_specs=[IN_VMEM] * 5,
            out_specs=IN_VMEM,
            out_shape=bf(2, 4, 2, PATCH, 256),
            compiler_params=PARAMS,
            cost_estimate=cost(10_000_000_000),
        )(tile, above, below, consts[0], consts[1])
        rims = pl.pallas_call(
            rims_kernel,
            in_specs=[IN_VMEM] * 4,
            out_specs=IN_VMEM,
            out_shape=bf(2, 4 * RIM, 640),
            compiler_params=PARAMS,
        )(above, below, left, right)
        return rims, inner

    def nothing(operands):
        return jnp.zeros((2, 4 * RIM, 640), jnp.bfloat16), jnp.zeros((2, 4, 2, PATCH, 256), jnp.bfloat16)

    rims, inner = lax.cond(
        row + col + gz < 99, around, nothing, (sections, above, below)
    )
    far = ring(rims, "gz", -1)
    outer = pl.pallas_call(
        outer_kernel,
        in_specs=[IN_VMEM] * 5,
        out_specs=IN_VMEM,
        out_shape=bf(2, 4, 2, PATCH, 256),
        scratch_shapes=[pltpu.VMEM((2, 640, 128), jnp.float32)],
        compiler_params=PARAMS,
        cost_estimate=cost(60_000_000_000),
    )(sections, rims, inner, consts[0], consts[1])
    later, outer = lax.optimization_barrier((sections, outer))
    lower = cut(later, [((1, 1), (a, b - a)) for a, b in zip(CUTS[:-1], CUTS[1:])])
    lower = [ring(part, "gz", -1) for part in lower]
    pairs = [(0, 1), (0, 2), (1, 2)]
    result, side = stage({0: first}, far, inner, outer, None, consts, (0,), pairs, 0)
    parts = {0: upper}
    spans = list(SPANS)
    if spans[0][0]:
        result, = stage(parts, far, inner, outer, (side, result), consts, (1,), [(1, 2)], 3, (0, spans[0][0]))
    for start, part, span in zip(CUTS, lower, spans):
        parts = {**parts, start: part}
        result, = stage(parts, far, inner, outer, (side, result), consts, (1,), [(1, 2)], 3, span)
    return result.reshape(2, 2, 4, 4, OFF * OFF)


def solution(mesh):
    return jax.shard_map(
        shards,
        mesh=mesh,
        in_specs=(P("gz", "row", "col"),),
        out_specs=P("gz", None, "row", "col", None),
        check_vma=False,
    )
```
